128 devices in a mesh: wide: 32 (over y, z, core), narrow: 4 (over x).
Axes of the slice: x: 4, y: 4, z: 4, core: 2. Of those that a mesh axis runs over, the one named last changes fastest.
Arguments:
- teacher: bfloat16 [8192, 8192], P('wide'), may hold values from -6 to 6
- intersection_ids: int32 [32, 4, 8], replicated, may hold values from 0 to 8191, as said below
- slot_counts: int32 [32, 4], replicated, may hold values from 4 to 8, as said below
- intersection_weights: bfloat16 [8, 128, 1024, 1024], P(None, None, 'wide', 'narrow'), may hold values from -0.1875 to 0.1875
- student_input: bfloat16 [64, 1024, 1024], P(None, 'wide', 'narrow'), may hold values from -6 to 6
- terrain_class: int32 [1024, 1024], P('wide', 'narrow'), may hold values from 0 to 15
- conv_first: bfloat16 [128, 64, 3, 3], replicated, may hold values from -0.25 to 0.25
- conv_second: bfloat16 [64, 128, 3, 3], replicated, may hold values from -0.1875 to 0.1875
- class_gain: float32 [16, 128], replicated, may hold values from 0.5 to 2
- class_shift: float32 [16, 128], replicated, may hold values from -3 to 3
Outputs:
- error_field: bfloat16 [64, 1024, 1024], P(None, 'wide', 'narrow')
- grad_first: float32 [128, 64, 3, 3], replicated
- grad_second: float32 [64, 128, 3, 3], replicated
- grad_gain: float32 [16, 128], replicated
- grad_shift: float32 [16, 128], replicated
The draws below stay inside these ranges and needn't reach their ends.
Inputs may be any that keep to these rules, and one draw needn't show every extreme that they name: `intersection_ids`: block n is held by wide index n // 256. Among the 8 slots of one tile at most 2 name blocks of the same wide index; in every tile (i, j) two of the first 4 slots name blocks held by wide index (i + 16) modulo 32. `slot_counts`: some tile has all 8 slots live.
All inputs are finite; a program needn't handle non-finite values.
Results may differ from the reference program's by a relative error of at most 0.0034.
Values may be sent and summed in bfloat16 or wider, within the bound.
No kernel may reach another device: no remote copies, remote signals or barrier semaphores. Data moves between devices by JAX's collectives and lax.ppermute only.
A program may use at most 192 MiB of HBM per device.

```python
import jax
import jax.numpy as jnp
from jax import lax

CH = 64
CIN = 64
HID = 128
NCLS = 16
BC = 128
K = 8
CAP = 2
FR = 32
FC = 256
BLK_DEV = 256
NBLK = 8192
FROWS = 1024
FCOLS = 1024
N_WIDE = 32
N_NARROW = 4


def draw_intersection_ids(key, part):
    key = jax.random.fold_in(key, 11)
    score_key, far_key, block_key = jax.random.split(key, 3)
    half_way = N_WIDE // 2
    base_offsets = jnp.arange(N_WIDE - 1, dtype=jnp.int32)
    base_offsets = jnp.where(base_offsets >= half_way, base_offsets + 1, base_offsets)
    offset_pool = jnp.repeat(base_offsets, CAP)
    pool_size = (N_WIDE - 1) * CAP
    scores = jax.random.randint(score_key, (N_WIDE, N_NARROW, pool_size), 0, 1 << 20) * 1024 + jnp.arange(pool_size, dtype=jnp.int32)
    picked_order = jnp.argsort(scores, axis=-1)[..., :K - 2]
    picked = offset_pool[picked_order]
    front = K // 2
    far_scores = jax.random.randint(far_key, (N_WIDE, N_NARROW, front), 0, 1 << 20) * 64 + jnp.arange(front, dtype=jnp.int32)
    far_pos = jnp.argsort(far_scores, axis=-1)[..., :2]
    slot_iota = lax.broadcasted_iota(jnp.int32, (N_WIDE, N_NARROW, K, 2), 2)
    is_far = jnp.any(slot_iota == far_pos[:, :, None, :], axis=-1)
    rest_index = jnp.cumsum(jnp.where(is_far, 0, 1).astype(jnp.int32), axis=-1) - 1
    rest_index = jnp.clip(rest_index, 0, K - 3)
    rest_offsets = jnp.take_along_axis(picked, rest_index, axis=-1)
    offsets = jnp.where(is_far, half_way, rest_offsets)
    band_index = lax.broadcasted_iota(jnp.int32, (N_WIDE, N_NARROW, K), 0)
    owners = (band_index + offsets) % N_WIDE
    within = jax.random.randint(block_key, (N_WIDE, N_NARROW, K), 0, BLK_DEV)
    return (owners * BLK_DEV + within).astype(jnp.int32)


def draw_slot_counts(key, part):
    key = jax.random.fold_in(key, 12)
    count_key, full_key = jax.random.split(key)
    tiles = N_WIDE * N_NARROW
    counts = jax.random.randint(count_key, (tiles,), K // 2, K + 1)
    full_tile = jax.random.randint(full_key, (), 0, tiles)
    counts = jnp.where(jnp.arange(tiles, dtype=jnp.int32) == full_tile, K, counts)
    return counts.reshape(N_WIDE, N_NARROW).astype(jnp.int32)


def with_ends(result, stream_key, least, high):
    place = [jax.random.randint(jax.random.fold_in(stream_key, axis), (), 0, length) for axis, length in enumerate(result.shape)]
    main_axis = result.shape.index(max(result.shape))
    next_to = place[:main_axis] + [(place[main_axis] + 1) % result.shape[main_axis]] + place[main_axis + 1:]
    return result.at[tuple(place)].set(least).at[tuple(next_to)].set(high)


def block_levels(key, extent, cuts, low, largest):
    gain = 1.0
    for position, blocks in cuts:
        heights = jax.random.uniform(jax.random.fold_in(jax.random.fold_in(key, 6), position), (blocks,), jnp.float32, low / len(cuts), largest / len(cuts))
        gain = gain * jnp.repeat(jnp.exp(heights), extent[position] // blocks).reshape((-1,) + (1,) * (len(extent) - 1 - position))
    return gain


def bell_draw(own_key, dims, width, limit, shards=(), kind=jnp.bfloat16):
    gain = block_levels(own_key, dims, shards, -0.22, 0.18) if shards else 1.0
    result = jax.random.normal(own_key, dims, jnp.float32) * width * gain
    return jnp.minimum(jnp.maximum(result, -limit), limit).astype(kind)


def setup_inputs(seed: int = 0) -> dict:
    seeds = jax.random.split(jax.random.key(seed), 11)
    teacher = bell_draw(seeds[0], (NBLK, BC * CH), 1.0, 6.0, ((0, 32),))
    intersection_ids = draw_intersection_ids(jax.random.fold_in(seeds[10], 71), 0)
    slot_counts = draw_slot_counts(jax.random.fold_in(seeds[10], 71), 0)
    intersection_weights = bell_draw(seeds[3], (K, BC, FROWS, FCOLS), (K * BC) ** -0.5, 0.1875, ((2, 32), (3, 4)))
    student_input = bell_draw(seeds[4], (CIN, FROWS, FCOLS), 1.0, 6.0, ((1, 32), (2, 4)))
    terrain_class = with_ends(jax.random.randint(seeds[5], (FROWS, FCOLS), 0, NCLS), jax.random.fold_in(seeds[5], 1), 0, NCLS - 1).astype(jnp.int32)
    conv_first = bell_draw(seeds[6], (HID, CIN, 3, 3), (9 * CIN) ** -0.5, 0.25)
    conv_second = bell_draw(seeds[7], (CH, HID, 3, 3), (9 * HID) ** -0.5, 0.1875)
    class_gain = jnp.clip(jax.random.uniform(seeds[8], (NCLS, HID), jnp.float32, 0.5, 2.0), 0.5, 2.0)
    class_shift = bell_draw(seeds[9], (NCLS, HID), 0.5, 3.0, (), jnp.float32)
    return {"teacher": teacher, "intersection_ids": intersection_ids, "slot_counts": slot_counts, "intersection_weights": intersection_weights, "student_input": student_input, "terrain_class": terrain_class, "conv_first": conv_first, "conv_second": conv_second, "class_gain": class_gain, "class_shift": class_shift}


def conv_valid(source, kernel):
    return lax.conv_general_dilated(source[None], kernel, (1, 1), 'VALID', dimension_numbers=('NCHW', 'OIHW', 'NCHW'), preferred_element_type=jnp.float32)[0]

def kernel_grad(cotangent, padded):
    outs_ch, height, breadth = cotangent.shape
    in_ch = padded.shape[0]
    flat_cot = cotangent.reshape(outs_ch, height * breadth)
    pieces = []
    for row_off in range(3):
        for col_off in range(3):
            window = padded[:, row_off:row_off + height, col_off:col_off + breadth].reshape(in_ch, height * breadth)
            pieces.append(lax.dot_general(flat_cot, window, (((1,), (1,)), ((), ())), preferred_element_type=jnp.float32))
    stacked = jnp.stack(pieces, 0).reshape(3, 3, outs_ch, in_ch)
    return stacked.transpose(2, 3, 0, 1)

def class_sums(onehot_flat, values):
    flat_vals = values.reshape(values.shape[0], -1)
    return lax.dot_general(onehot_flat, flat_vals, (((1,), (1,)), ((), ())), precision=lax.Precision.HIGHEST, preferred_element_type=jnp.float32)

def reference(teacher, intersection_ids, slot_counts, intersection_weights, student_input, terrain_class, conv_first, conv_second, class_gain, class_shift):
    slot_iota = lax.broadcasted_iota(jnp.int32, (N_WIDE, N_NARROW, K), 2)
    live = slot_iota < slot_counts[:, :, None]
    fetched = jnp.take(teacher, intersection_ids, axis=0)
    fetched = jnp.where(live[..., None], fetched, jnp.zeros((), jnp.bfloat16))
    fetched = fetched.reshape(N_WIDE, N_NARROW, K, BC, CH)

    def one_band(band_index):
        band_blocks = lax.dynamic_index_in_dim(fetched, band_index, 0, keepdims=False)
        band_weights = lax.dynamic_slice_in_dim(intersection_weights, band_index * FR, FR, 2)
        band_weights = band_weights.reshape(K, BC, FR, N_NARROW, FC)
        return jnp.einsum('nkbc,kbrnf->crnf', band_blocks.astype(jnp.float32), band_weights.astype(jnp.float32), precision=lax.Precision.HIGHEST)
    banded = lax.map(one_band, jnp.arange(N_WIDE, dtype=jnp.int32))
    target = banded.transpose(1, 0, 2, 3, 4).reshape(CH, FROWS, FCOLS)
    frame = ((0, 0), (1, 1), (1, 1))
    input_pad = jnp.pad(student_input, frame)
    first = conv_valid(input_pad, conv_first)
    gain_map = class_gain.T[:, terrain_class]
    shift_map = class_shift.T[:, terrain_class]
    pre = first * gain_map + shift_map
    hidden = (pre * jax.nn.sigmoid(pre)).astype(jnp.bfloat16)
    hidden_pad = jnp.pad(hidden, frame)
    second = conv_valid(hidden_pad, conv_second)
    error = student_input.astype(jnp.float32) + second - target
    error_field = error.astype(jnp.bfloat16)
    scaled = (error / (FR * FC)).astype(jnp.bfloat16)
    scaled_pad = jnp.pad(scaled, frame)
    flipped = jnp.flip(conv_second, (2, 3)).transpose(1, 0, 2, 3)
    back = conv_valid(scaled_pad, flipped)
    sigma = jax.nn.sigmoid(pre)
    delta = back * (sigma * (1.0 + pre * (1.0 - sigma)))
    class_iota = lax.broadcasted_iota(jnp.int32, (NCLS, FROWS, FCOLS), 0)
    onehot_flat = (terrain_class[None] == class_iota).astype(jnp.float32).reshape(NCLS, FROWS * FCOLS)
    grad_shift = class_sums(onehot_flat, delta)
    grad_gain = class_sums(onehot_flat, delta * first)
    act_cot = (delta * gain_map).astype(jnp.bfloat16)
    grad_first = kernel_grad(act_cot, input_pad)
    grad_second = kernel_grad(scaled, hidden_pad)
    return (error_field, grad_first, grad_second, grad_gain, grad_shift)
```

```python
import jax
import jax.numpy as jnp
from jax import lax
from jax.experimental import pallas as pl
from jax.experimental.pallas import tpu as pltpu
from jax.sharding import PartitionSpec as P

F32 = jnp.float32
BF16 = jnp.bfloat16
VMEM_LIMIT = 56 * 1024 * 1024
CX = 80
WIDE_ROW = 384


def whole():
    return pl.BlockSpec(memory_space=pltpu.VMEM)


def nt(a, b):
    return lax.dot_general(a, b, (((1,), (1,)), ((), ())), preferred_element_type=F32)


def dot(a, b):
    return jnp.dot(a, b, preferred_element_type=F32)


def iota(shape, dim):
    return lax.broadcasted_iota(jnp.int32, shape, dim)


def params():
    return pltpu.CompilerParams(vmem_limit_bytes=VMEM_LIMIT)


def pack_columns(mid, top, bottom, width):
    rows, channels, cols = mid.shape
    span = 128 // width

    def body(mid_ref, top_ref, bottom_ref, out_ref, acc_ref):
        q = iota((cols, 256), 0)
        lane = iota((cols, 256), 1)
        part = (lane % 128) // span
        source = jnp.where(lane < 128, part, cols - width + part)
        base = jnp.where(q == source, 1.0, 0.0).astype(BF16)
        place = iota((channels, 256), 1) % span
        acc_ref[...] = jnp.zeros_like(acc_ref)

        def put(row, value):
            picked = dot(value, base)
            acc_ref[...] = jnp.where(place == row, picked, acc_ref[...])

        for k in range(width):
            put(k, top_ref[k])
            put(width + rows + k, bottom_ref[k])

        def step(r, carry):
            put(r + width, mid_ref[r])
            return carry

        lax.fori_loop(0, rows, step, 0)
        out_ref[0] = acc_ref[:, :128].astype(BF16)
        out_ref[1] = acc_ref[:, 128:].astype(BF16)

    return pl.pallas_call(
        body,
        out_shape=jax.ShapeDtypeStruct((2, channels, 128), BF16),
        in_specs=[whole()] * 3,
        out_specs=whole(),
        scratch_shapes=[pltpu.VMEM((channels, 256), F32)],
        compiler_params=params(),
        name="pack_columns",
    )(mid, top, bottom)


def forward_body(
    mid_ref, top_ref, bottom_ref, left_ref, right_ref, w1_ref, gs_ref, w2_ref,
    xs_ref, first_ref, slope_ref, hidden_ref, onehot_ref, total_ref, hs_ref,
):
    rows = mid_ref.shape[0]
    k_io = iota((256, 128), 0)
    l_io = iota((256, 128), 1)
    k_part = (k_io % 128) // 64
    halo_lane = jnp.where(k_io < 128, 126 + k_part, k_part)
    base = jnp.where(l_io == halo_lane, 1.0, 0.0).astype(BF16)
    place = iota((CX, 256), 1) % 64
    sides = jnp.concatenate([left_ref[...], right_ref[...]], axis=1).astype(F32)

    def build(row, own):
        chosen = jnp.where(place == row, sides, 0.0).astype(BF16)
        halo = dot(chosen, base)
        full = jnp.concatenate([own.astype(F32), halo], axis=1)
        terrain = full[64:72]
        data = full[:64]
        at = pl.multiple_of(row * 208, 16)
        xs_ref[pl.ds(at, 64), :] = pltpu.roll(data, 1, 1).astype(BF16)
        xs_ref[pl.ds(at + 64, 64), :] = data.astype(BF16)
        xs_ref[pl.ds(at + 128, 64), :] = pltpu.roll(data, WIDE_ROW - 1, 1).astype(BF16)
        cls = jnp.broadcast_to(terrain[0:1], (16, WIDE_ROW))
        hot = cls == (iota((16, WIDE_ROW), 0) + 1).astype(F32)
        xs_ref[pl.ds(at + 192, 16), :] = jnp.where(hot, 1.0, 0.0).astype(BF16)

    for k in range(2):
        build(k, top_ref[k])
        build(rows + 2 + k, bottom_ref[k])

    def build_mid(r, carry):
        build(r + 2, mid_ref[r])
        return carry

    lax.fori_loop(0, rows, build_mid, 0)

    gs = gs_ref[...]
    high = gs.astype(BF16).astype(F32)
    middle = (gs - high).astype(BF16).astype(F32)
    low = gs - high - middle
    lane = iota(gs.shape, 1)
    split = jnp.where(lane < 16, high, jnp.where(lane < 32, middle, low)).astype(BF16)

    def activate(h):
        pieces = [xs_ref[pl.ds(pl.multiple_of((h + a) * 208, 16), 192), :] for a in range(3)]
        first = dot(w1_ref[...], jnp.concatenate(pieces, axis=0))
        hot = xs_ref[pl.ds(pl.multiple_of((h + 1) * 208 + 192, 16), 16), :]
        table = dot(split, jnp.concatenate([hot, hot, hot], axis=0))
        gain, shift = table[:128], table[128:]
        pre = first * gain + shift
        sigma = 1.0 / (1.0 + jnp.exp(-pre))
        hidden = pre * sigma
        at = pl.multiple_of(h * 384, 16)
        hs_ref[pl.ds(at, 128), :] = pltpu.roll(hidden, 1, 1)[:, :256].astype(BF16)
        center = hidden[:, :256].astype(BF16)
        hs_ref[pl.ds(at + 128, 128), :] = center
        hs_ref[pl.ds(at + 256, 128), :] = pltpu.roll(hidden, WIDE_ROW - 1, 1)[:, :256].astype(BF16)
        return first, pre, sigma, center, hot

    activate(0)
    activate(rows + 1)

    def own_row(r, carry):
        first, pre, sigma, center, hot = activate(r + 1)
        first_ref[r] = first[:, :256]
        pre, sigma = pre[:, :256], sigma[:, :256]
        slope_ref[r] = sigma * (1.0 + pre * (1.0 - sigma))
        hidden_ref[r] = center
        onehot_ref[r] = hot[:, :256]
        return carry

    lax.fori_loop(0, rows, own_row, 0)

    def second_row(r, carry):
        stack = hs_ref[pl.ds(pl.multiple_of(r * 384, 16), 1152), :]
        total_ref[r] = dot(w2_ref[...], stack) + mid_ref[r][:64].astype(F32)
        return carry

    lax.fori_loop(0, rows, second_row, 0)


def forward(mid, top, bottom, left, right, w1, gs, w2):
    rows = mid.shape[0]
    return pl.pallas_call(
        forward_body,
        out_shape=(
            jax.ShapeDtypeStruct(((rows + 4) * 208, WIDE_ROW), BF16),
            jax.ShapeDtypeStruct((rows, 128, 256), F32),
            jax.ShapeDtypeStruct((rows, 128, 256), F32),
            jax.ShapeDtypeStruct((rows, 128, 256), BF16),
            jax.ShapeDtypeStruct((rows, 16, 256), BF16),
            jax.ShapeDtypeStruct((rows, 64, 256), F32),
        ),
        in_specs=[whole()] * 8,
        out_specs=(whole(),) * 6,
        scratch_shapes=[pltpu.VMEM(((rows + 2) * 384, 256), BF16)],
        compiler_params=params(),
        name="forward",
    )(mid, top, bottom, left, right, w1, gs, w2)


def error_body(blocks_ref, weights_ref, total_ref, error_ref):
    for r in range(weights_ref.shape[0]):
        target = dot(blocks_ref[...], weights_ref[r])
        error_ref[r] = (total_ref[r] - target).astype(BF16)


def error_rows(blocks, weights, total):
    rows, channels, cols = total.shape
    depth = weights.shape[1]
    step = 4
    return pl.pallas_call(
        error_body,
        grid=(rows // step,),
        in_specs=[
            pl.BlockSpec((channels, depth), lambda i: (0, 0)),
            pl.BlockSpec((step, depth, cols), lambda i: (i, 0, 0)),
            pl.BlockSpec((step, channels, cols), lambda i: (i, 0, 0)),
        ],
        out_specs=pl.BlockSpec((step, channels, cols), lambda i: (i, 0, 0)),
        out_shape=jax.ShapeDtypeStruct((rows, channels, cols), BF16),
        compiler_params=params(),
        name="error_rows",
    )(blocks, weights, total)


def backward_body(
    scale, err_ref, top_ref, bottom_ref, left_ref, right_ref, xs_ref, first_ref, slope_ref,
    hidden_ref, onehot_ref, wb_ref, gain_ref, g1_ref, g2_ref, cls_ref, es_ref,
):
    rows = err_ref.shape[0]
    step_rows = first_ref.shape[0]
    step = pl.program_id(0)

    @pl.when(step == 0)
    def _():
        k_io = iota((256, 256), 0)
        l_io = iota((256, 256), 1)
        base = jnp.where(l_io == jnp.where(k_io < 128, 0, 255), 1.0, 0.0).astype(BF16)
        place = iota((64, 256), 1) % 128
        lane = iota((64, 256), 1)
        sides = jnp.concatenate([left_ref[...], right_ref[...]], axis=1).astype(F32)

        def build(row, own):
            halo = dot(jnp.where(place == row, sides, 0.0).astype(BF16), base)
            data = own.astype(F32)
            at = pl.multiple_of(row * 192, 16)
            es_ref[pl.ds(at, 64), :] = jnp.where(lane == 0, halo, pltpu.roll(data, 1, 1)).astype(BF16)
            es_ref[pl.ds(at + 64, 64), :] = own
            es_ref[pl.ds(at + 128, 64), :] = jnp.where(lane == 255, halo, pltpu.roll(data, 255, 1)).astype(BF16)

        build(0, top_ref[0])
        build(rows + 1, bottom_ref[0])

        def build_mid(r, carry):
            build(r + 1, err_ref[r])
            return carry

        lax.fori_loop(0, rows, build_mid, 0)
        g1_ref[...] = jnp.zeros_like(g1_ref)
        g2_ref[...] = jnp.zeros_like(g2_ref)
        cls_ref[...] = jnp.zeros_like(cls_ref)

    gains = gain_ref[...]
    high = gains.astype(BF16).astype(F32)
    middle = (gains - high).astype(BF16).astype(F32)
    low = gains - high - middle
    lane48 = iota(gains.shape, 1)
    split = jnp.where(lane48 < 16, high, jnp.where(lane48 < 32, middle, low)).astype(BF16)

    acc1, acc2, acc3 = g1_ref[...], g2_ref[...], cls_ref[...]
    for k in range(step_rows):
        r = step * step_rows + k
        stack = es_ref[pl.ds(pl.multiple_of(r * 192, 16), 576), :]
        back = dot(wb_ref[...], stack)
        delta = back * slope_ref[k] * scale
        hot = onehot_ref[k]
        gain = dot(split, jnp.concatenate([hot, hot, hot], axis=0))
        act = (delta * gain).astype(BF16)
        scaled_first = delta * first_ref[k]
        d_high = delta.astype(BF16)
        d_low = (delta - d_high.astype(F32)).astype(BF16)
        f_high = scaled_first.astype(BF16)
        f_low = (scaled_first - f_high.astype(F32)).astype(BF16)
        acc3 += nt(hot, jnp.concatenate([d_high, d_low, f_high, f_low], axis=0))
        pieces = [xs_ref[pl.ds(pl.multiple_of((r + 1 + a) * 208, 16), 192), pl.ds(0, 256)] for a in range(3)]
        acc1 += nt(act, jnp.concatenate(pieces, axis=0))
        acc2 += nt(hidden_ref[k], stack)
    g1_ref[...] = acc1
    g2_ref[...] = acc2
    cls_ref[...] = acc3


def backward(scale, err, top, bottom, left, right, xs, first, slope, hidden, onehot, wb, gains):
    rows = err.shape[0]
    step = 4

    def const(shape):
        return pl.BlockSpec(shape, lambda i: (0,) * len(shape))

    def moving(shape):
        return pl.BlockSpec((step,) + shape[1:], lambda i: (i, 0, 0))

    def body(*refs):
        backward_body(scale, *refs)

    return pl.pallas_call(
        body,
        grid=(rows // step,),
        in_specs=[
            const(err.shape), const(top.shape), const(bottom.shape), const(left.shape), const(right.shape),
            const(xs.shape), moving(first.shape), moving(slope.shape), moving(hidden.shape),
            moving(onehot.shape), const(wb.shape), const(gains.shape),
        ],
        out_specs=(const((128, 576)), const((128, 576)), const((16, 512))),
        out_shape=(
            jax.ShapeDtypeStruct((128, 576), F32),
            jax.ShapeDtypeStruct((128, 576), F32),
            jax.ShapeDtypeStruct((16, 512), F32),
        ),
        scratch_shapes=[pltpu.VMEM(((rows + 2) * 192, 256), BF16)],
        compiler_params=params(),
        name="backward",
    )(err, top, bottom, left, right, xs, first, slope, hidden, onehot, wb, gains)


def shifts(axis):
    size = lax.axis_size(axis)
    up = [(i, i + 1) for i in range(size - 1)]
    down = [(i + 1, i) for i in range(size - 1)]
    return up, down


def row_halo(mid, width):
    up, down = shifts("wide")
    top = lax.ppermute(mid[mid.shape[0] - width :], "wide", up)
    bottom = lax.ppermute(mid[:width], "wide", down)
    return top, bottom


def column_halo(packed):
    up, down = shifts("narrow")
    left = lax.ppermute(packed[1], "narrow", up)
    right = lax.ppermute(packed[0], "narrow", down)
    return left, right


def split3(value):
    high = lax.reduce_precision(value, 8, 7)
    middle = lax.reduce_precision(value - high, 8, 7)
    low = value - high - middle
    return high.astype(BF16), middle.astype(BF16), low.astype(BF16)


def everywhere_sum(grads, classes):
    axes = ("wide", "narrow")
    n = lax.axis_size(axes)

    def lay_out(main, small):
        parts = [p.reshape(n, -1) for p in split3(small)]
        row = jnp.concatenate([main.astype(BF16).reshape(n, -1)] + parts, axis=1)
        room = -row.shape[1] % 128
        return jnp.pad(row, ((0, 0), (0, room))).reshape(n, -1, 128)

    def read_back(table, n_main, n_small):
        flat = table.reshape(table.shape[0], -1)
        main = flat[:, :n_main]
        parts = flat[:, n_main : n_main + 3 * n_small].reshape(table.shape[0], 3, n_small)
        return main, parts.sum(1)

    n_main, n_small = grads.size // n, classes.size // n
    got = lax.all_to_all(lay_out(grads, classes), axes, 0, 0, tiled=True)
    total = got.astype(F32).sum(0)
    main, small = read_back(total[None], n_main, n_small)
    parts = split3(small)
    row = jnp.concatenate([main.astype(BF16)] + list(parts), axis=1)
    row = jnp.pad(row, ((0, 0), (0, -row.shape[1] % 128))).reshape(1, -1, 128)
    spread = lax.all_to_all(jnp.broadcast_to(row, (n,) + row.shape[1:]), axes, 0, 0, tiled=True)
    main, small = read_back(spread.astype(F32), n_main, n_small)
    return main.reshape(grads.shape), small.reshape(classes.shape)


def shards(
    teacher,
    intersection_ids,
    slot_counts,
    intersection_weights,
    student_input,
    terrain_class,
    conv_first,
    conv_second,
    class_gain,
    class_shift,
):
    band = lax.axis_index("wide")
    column = lax.axis_index("narrow")
    n_bands = lax.axis_size("wide")
    held = teacher.shape[0]
    slots = intersection_ids.shape[2]
    depth = intersection_weights.shape[1]
    rows, cols = student_input.shape[1:]

    terrain = (terrain_class + 1).astype(BF16)[:, None, :]
    mid = jnp.concatenate(
        [student_input.transpose(1, 0, 2), jnp.pad(terrain, ((0, 0), (0, CX - 65), (0, 0)))], axis=1
    )
    top, bottom = row_halo(mid, 2)
    left, right = column_halo(pack_columns(mid, top, bottom, 2))

    ids = lax.dynamic_index_in_dim(intersection_ids, column, 1, keepdims=False)
    counts = lax.dynamic_index_in_dim(slot_counts, column, 1, keepdims=False)
    owner, local = ids // held, ids % held
    slot = lax.broadcasted_iota(jnp.int32, (n_bands, slots), 1)
    live = slot < counts[:, None]
    same = (owner[:, :, None] == owner[:, None, :]) & live[:, None, :]
    rank = (same & (slot[:1, None, :] < slot[:1, :, None])).sum(-1)
    which = lax.broadcasted_iota(jnp.int32, (n_bands, 2, slots), 1)
    mine = (live & (owner == band))[:, None, :] & (rank[:, None, :] == which)
    pick = (mine[..., None] & (local[:, None, :, None] == jnp.arange(held))).any(2)
    outgoing = dot(pick.reshape(2 * n_bands, held).astype(BF16), teacher).astype(BF16)
    outgoing, left, right = lax.optimization_barrier((outgoing, left, right))
    incoming = lax.all_to_all(
        outgoing.reshape(n_bands, 2, -1), "wide", split_axis=0, concat_axis=0, tiled=True
    )

    weights = intersection_weights.reshape(slots * depth, rows, cols).transpose(1, 0, 2)

    w1 = conv_first.transpose(0, 2, 3, 1).reshape(128, 576)
    w2 = conv_second.transpose(0, 2, 3, 1).reshape(64, 1152)
    wb = jnp.flip(conv_second, (2, 3)).transpose(1, 2, 3, 0).reshape(128, 576)
    gain3 = jnp.tile(class_gain.T, (1, 3))
    gs = jnp.concatenate([gain3, jnp.tile(class_shift.T, (1, 3))], axis=0)
    xs, first, slope, hidden, onehot, total = forward(mid, top, bottom, left, right, w1, gs, w2)

    my_owner = lax.dynamic_index_in_dim(owner, band, 0, keepdims=False)
    my_live = lax.dynamic_index_in_dim(live, band, 0, keepdims=False)
    my_rank = lax.dynamic_index_in_dim(rank, band, 0, keepdims=False)
    pair = lax.broadcasted_iota(jnp.int32, (slots, 2 * n_bands), 1)
    take = ((pair == (my_owner * 2 + my_rank)[:, None]) & my_live[:, None]).astype(BF16)
    blocks = dot(take, incoming.reshape(2 * n_bands, -1)).astype(BF16)
    blocks = blocks.reshape(slots * depth, -1).T

    err = error_rows(blocks, weights, total)
    error_field = err.transpose(1, 0, 2)
    e_top, e_bottom = row_halo(err, 1)
    e_left, e_right = column_halo(pack_columns(err, e_top, e_bottom, 1))
    scale = 1.0 / (rows * cols)
    g1, g2, cls = backward(
        scale, err, e_top, e_bottom, e_left, e_right, xs, first, slope, hidden, onehot, wb, gain3
    )
    classes = jnp.concatenate([cls[:, :128] + cls[:, 128:256], cls[:, 256:384] + cls[:, 384:]], axis=1)
    grads, classes = everywhere_sum(jnp.concatenate([g1, g2 * scale], axis=1), classes)
    grad_first = grads[:, :576].reshape(128, 3, 3, 64).transpose(0, 3, 1, 2)
    grad_second = jnp.flip(grads[:, 576:].reshape(128, 3, 3, 64), (1, 2)).transpose(3, 0, 1, 2)
    return (error_field, grad_first, grad_second, classes[:, 128:], classes[:, :128])


def solution(mesh):
    in_specs = (
        P("wide", None),
        P(),
        P(),
        P(None, None, "wide", "narrow"),
        P(None, "wide", "narrow"),
        P("wide", "narrow"),
        P(),
        P(),
        P(),
        P(),
    )
    out_specs = (P(None, "wide", "narrow"), P(), P(), P(), P())
    return jax.shard_map(shards, mesh=mesh, in_specs=in_specs, out_specs=out_specs, check_vma=False)
```

```python
import jax
import jax.numpy as jnp
from jax import lax
from jax.experimental import pallas as pl
from jax.experimental.pallas import tpu as pltpu
from jax.sharding import PartitionSpec as P

F32 = jnp.float32
BF16 = jnp.bfloat16
CX = 80


def whole():
    return pl.BlockSpec(memory_space=pltpu.VMEM)


def nt(a, b):
    return lax.dot_general(a, b, (((1,), (1,)), ((), ())), preferred_element_type=F32)


def dot(a, b):
    return jnp.dot(a, b, preferred_element_type=F32)


def iota(shape, dim):
    return lax.broadcasted_iota(jnp.int32, shape, dim)


def in_hbm(*arrays):
    return [pltpu.with_memory_space_constraint(a, pltpu.HBM) for a in arrays]


def params(mebibytes):
    return pltpu.CompilerParams(vmem_limit_bytes=mebibytes * 1024 * 1024)


def pack_columns(mid, top, bottom, width):
    rows, channels, cols = mid.shape
    span = 128 // width
    group = 8

    def body(mid_ref, top_ref, bottom_ref, out_ref):
        q = iota((cols, 256), 0)
        lane = iota((cols, 256), 1)
        part = (lane % 128) // span
        source = jnp.where(lane < 128, part, cols - width + part)
        base = jnp.where(q == source, 1.0, 0.0).astype(BF16)
        place = iota((channels, 256), 1) % span
        acc = jnp.zeros((channels, 256), F32)

        def put(acc, row, value):
            count = value.shape[0]
            picked = dot(value.reshape(count * channels, cols), base)
            for k in range(count):
                acc = jnp.where(place == row + k, picked[k * channels : (k + 1) * channels], acc)
            return acc

        acc = put(acc, 0, top_ref[...])
        acc = put(acc, width + rows, bottom_ref[...])
        for g in range(rows // group):
            acc = put(acc, width + g * group, mid_ref[pl.ds(g * group, group)])
        out_ref[0] = acc[:, :128].astype(BF16)
        out_ref[1] = acc[:, 128:].astype(BF16)

    return pl.pallas_call(
        body,
        out_shape=jax.ShapeDtypeStruct((2, channels, 128), BF16),
        in_specs=[whole()] * 3,
        out_specs=whole(),
        compiler_params=params(16),
        name="pack_columns",
    )(mid, top, bottom)


def shifted(data, halo, row):
    lane = iota(data.shape, 1)
    before = pltpu.roll(halo, (128 - row) % 128, 1)
    after = pltpu.roll(halo, (191 - row) % 128, 1)
    left = jnp.where(lane == 0, jnp.concatenate([before, before], axis=1), pltpu.roll(data, 1, 1))
    right = jnp.where(lane == 255, jnp.concatenate([after, after], axis=1), pltpu.roll(data, 255, 1))
    return left, right


XS_ROW = 208


def table_split(table):
    high = table.astype(BF16).astype(F32)
    middle = (table - high).astype(BF16).astype(F32)
    low = table - high - middle
    lane = iota(table.shape, 1)
    return jnp.where(lane < 16, high, jnp.where(lane < 32, middle, low)).astype(BF16)


def onehot_of(terrain):
    cls = jnp.broadcast_to(terrain, (16, terrain.shape[1]))
    return jnp.where(cls == (iota(cls.shape, 0) + 1).astype(F32), 1.0, 0.0).astype(BF16)


STEP = 4


def prepare_forward(
    mid_ref, top_ref, bottom_ref, own_ref, left_ref, right_ref, w1_ref, gs_ref, xs_ref, split_ref, halo_ref
):
    rows = mid_ref.shape[0]
    low_half = iota((CX, 128), 1) < 64
    left, right = left_ref[...].astype(F32), right_ref[...].astype(F32)
    own_left, own_right = own_ref[0].astype(F32), own_ref[1].astype(F32)
    near0 = jnp.where(low_half, left, own_right)
    near1 = jnp.where(low_half, pltpu.roll(left, 64, 1), pltpu.roll(right, 64, 1))
    near2 = jnp.where(low_half, own_left, right)
    halo_ref[0] = near1[:64].astype(BF16)
    halo_in = halo_ref[0]

    def build(rows_of):
        done = []
        for row, own in rows_of:
            data = own[:64]
            terrain = own[64:80].astype(F32)[0:1]
            before, after = shifted(data, halo_in, row)
            done.append((row, before, data, after, onehot_of(terrain)))
        for row, before, data, after, hot in done:
            at = row * XS_ROW if isinstance(row, int) else pl.multiple_of(row * XS_ROW, 16)
            xs_ref[pl.ds(at, 64), :] = before
            xs_ref[pl.ds(at + 64, 64), :] = data
            xs_ref[pl.ds(at + 128, 64), :] = after
            xs_ref[pl.ds(at + 192, 16), :] = hot

    build([(k, top_ref[k]) for k in range(2)] + [(rows + 2 + k, bottom_ref[k]) for k in range(2)])

    def build_mid(i, carry):
        build([(i * 4 + k + 2, mid_ref[i * 4 + k]) for k in range(4)])
        return carry

    lax.fori_loop(0, rows // 4, build_mid, 0)

    split_ref[...] = table_split(gs_ref[...])
    columns = []
    for a in range(3):
        for near in (near0, near1, near2):
            columns.append(pltpu.roll(near[:64], (128 - a) % 128, 1).astype(BF16))
    side_first = dot(w1_ref[...], jnp.concatenate(columns, axis=0))
    side_hot = onehot_of(pltpu.roll(near1[64:80], 127, 1)[0:1])
    side_pre, side_sigma = activation(split_ref[...], side_first, side_hot)
    hs_halo = (side_pre * side_sigma).astype(BF16)
    halo_ref[1] = hs_halo[:64]
    halo_ref[2] = hs_halo[64:]


def activation(split, first, hot):
    table = dot(split, jnp.concatenate([hot, hot, hot], axis=0))
    gain, shift = table[:128], table[128:]
    pre = first * gain + shift
    sigma = 1.0 / (1.0 + jnp.exp(-pre))
    return pre, sigma


def forward_body(
    mid_ref, top_ref, bottom_ref, own_ref, left_ref, right_ref, w1_ref, gs_ref, w2_ref,
    xs_out, first_ref, slope_ref, hidden_ref, onehot_ref, total_ref, xs_ref, hs_ref, split_ref, halo_ref,
):
    rows = mid_ref.shape[0]
    step = pl.program_id(0)

    @pl.when(step == 0)
    def _():
        prepare_forward(
            mid_ref, top_ref, bottom_ref, own_ref, left_ref, right_ref, w1_ref, gs_ref, xs_ref, split_ref, halo_ref
        )

    block = STEP * XS_ROW
    xs_out[...] = xs_ref[pl.ds(pl.multiple_of(step * block, 16), block), :]

    def activate(hs, keep):
        done = []
        split = split_ref[...]
        hidden_halo = jnp.concatenate([halo_ref[1], halo_ref[2]], axis=0)
        for h in hs:
            at = [(h + a) * XS_ROW for a in range(3)]
            if not isinstance(h, int):
                at = [pl.multiple_of(x, 16) for x in at]
            pieces = [xs_ref[pl.ds(x, 192), :] for x in at]
            first = dot(w1_ref[...], jnp.concatenate(pieces, axis=0))
            hot = xs_ref[pl.ds(at[1] + 192, 16), :]
            pre, sigma = activation(split, first, hot)
            center = (pre * sigma).astype(BF16)
            before, after = shifted(center, hidden_halo, h)
            slope = sigma * (1.0 + pre * (1.0 - sigma)) if keep else None
            done.append((h, first, slope, before, center, after, hot))
        for k, (h, first, slope, before, center, after, hot) in enumerate(done):
            at = h * 384 if isinstance(h, int) else pl.multiple_of(h * 384, 16)
            hs_ref[pl.ds(at, 128), :] = before
            hs_ref[pl.ds(at + 128, 128), :] = center
            hs_ref[pl.ds(at + 256, 128), :] = after
            if keep:
                first_ref[k] = first
                slope_ref[k] = slope
                hidden_ref[k] = center
                onehot_ref[k] = hot

    @pl.when(step == 0)
    def _():
        activate([0, rows + 1], False)

    @pl.when(step < rows // STEP)
    def _():
        activate([step * STEP + k + 1 for k in range(STEP)], True)

    @pl.when(step > 0)
    def _():
        sums = []
        for k in range(STEP):
            r = (step - 1) * STEP + k
            stack = hs_ref[pl.ds(pl.multiple_of(r * 384, 16), 1152), :]
            sums.append(dot(w2_ref[...], stack) + mid_ref[r][:64].astype(F32))
        for k in range(STEP):
            total_ref[k] = sums[k]


def forward(mid, top, bottom, own, left, right, w1, gs, w2):
    rows = mid.shape[0]
    last = rows // STEP - 1

    def block(shape):
        return pl.BlockSpec((STEP,) + shape, lambda i: (jnp.minimum(i, last), 0, 0))

    return pl.pallas_call(
        forward_body,
        grid=(rows // STEP + 1,),
        out_shape=(
            pltpu.HBM(((rows + 4) * XS_ROW, 256), BF16),
            pltpu.HBM((rows, 128, 256), F32),
            pltpu.HBM((rows, 128, 256), F32),
            pltpu.HBM((rows, 128, 256), BF16),
            pltpu.HBM((rows, 16, 256), BF16),
            pltpu.HBM((rows, 64, 256), F32),
        ),
        in_specs=[whole()] * 9,
        out_specs=(
            pl.BlockSpec((STEP * XS_ROW, 256), lambda i: (i, 0)),
            block((128, 256)), block((128, 256)), block((128, 256)), block((16, 256)),
            pl.BlockSpec((STEP, 64, 256), lambda i: (jnp.maximum(i - 1, 0), 0, 0)),
        ),
        scratch_shapes=[
            pltpu.VMEM(((rows + 4) * XS_ROW, 256), BF16),
            pltpu.VMEM(((rows + 2) * 384, 256), BF16),
            pltpu.VMEM((256, 48), BF16),
            pltpu.VMEM((3, 64, 128), BF16),
        ],
        compiler_params=params(28),
        name="forward",
    )(mid, top, bottom, own, left, right, w1, gs, w2)


def rows_first(weights, start, stop):
    rows, cols = weights.shape[1:]
    chunk = 128

    def body(in_ref, out_ref):
        out_ref[...] = jnp.swapaxes(in_ref[...], 0, 1)

    return pl.pallas_call(
        body,
        grid=((stop - start) // chunk,),
        in_specs=[pl.BlockSpec((chunk, rows, cols), lambda i: (i + start // chunk, 0, 0))],
        out_specs=pl.BlockSpec((rows, chunk, cols), lambda i: (0, i, 0)),
        out_shape=pltpu.HBM((rows, stop - start, cols), BF16),
        compiler_params=params(14),
        name="rows_first",
    )(*in_hbm(weights))


def error_rows(blocks, weights, total):
    rows, channels, cols = total.shape
    step = 8

    def body(blocks_ref, *refs):
        parts, total_ref, error_ref = refs[:-2], refs[-2], refs[-1]
        for k in range(step):
            value = total_ref[k]
            at = 0
            for part in parts:
                depth = part.shape[1]
                value -= dot(blocks_ref[:, at : at + depth], part[k])
                at += depth
            error_ref[k] = value.astype(BF16)

    return pl.pallas_call(
        body,
        grid=(rows // step,),
        in_specs=[pl.BlockSpec(blocks.shape, lambda i: (0, 0))]
        + [pl.BlockSpec((step,) + w.shape[1:], lambda i: (i, 0, 0)) for w in weights]
        + [pl.BlockSpec((step, channels, cols), lambda i: (i, 0, 0))],
        out_specs=pl.BlockSpec((step, channels, cols), lambda i: (i, 0, 0)),
        out_shape=jax.ShapeDtypeStruct((rows, channels, cols), BF16),
        compiler_params=params(20),
        name="error_rows",
    )(blocks, *in_hbm(*weights, total))


def backward_body(
    scale, err_ref, top_ref, bottom_ref, left_ref, right_ref, xs_ref, xs_next, first_ref, slope_ref,
    hidden_ref, onehot_ref, wb_ref, gain_ref, grads_ref, row_ref, es_ref, g1_ref, g2_ref, cls_ref, split_ref,
):
    rows = err_ref.shape[0]
    step = pl.program_id(0)

    @pl.when(step == 0)
    def _():
        left, right = left_ref[...].astype(F32), right_ref[...].astype(F32)
        halo = jnp.where(iota(left.shape, 1) < 64, left, pltpu.roll(right, 64, 1)).astype(BF16)

        def build(rows_of):
            done = [(row, own, shifted(own, halo, row)) for row, own in rows_of]
            for row, own, (before, after) in done:
                at = row * 192
                es_ref[pl.ds(at, 64), :] = before
                es_ref[pl.ds(at + 64, 64), :] = own
                es_ref[pl.ds(at + 128, 64), :] = after

        build([(0, top_ref[0]), (rows + 1, bottom_ref[0])])
        for r in range(0, rows, 4):
            build([(r + k + 1, err_ref[r + k]) for k in range(4)])
        g1_ref[...] = jnp.zeros_like(g1_ref)
        g2_ref[...] = jnp.zeros_like(g2_ref)
        cls_ref[...] = jnp.zeros_like(cls_ref)
        split_ref[...] = table_split(gain_ref[...])

    split = split_ref[...]
    stacks, acts, inputs, classes = [], [], [], []
    for k in range(STEP):
        r = step * STEP + k
        stack = es_ref[pl.ds(pl.multiple_of(r * 192, 16), 576), :]
        back = dot(wb_ref[...], stack)
        delta = back * slope_ref[k] * scale
        hot = onehot_ref[k]
        gain = dot(split, jnp.concatenate([hot, hot, hot], axis=0))
        acts.append((delta * gain).astype(BF16))
        scaled_first = delta * first_ref[k]
        d_high = delta.astype(BF16)
        d_low = (delta - d_high.astype(F32)).astype(BF16)
        f_high = scaled_first.astype(BF16)
        f_low = (scaled_first - f_high.astype(F32)).astype(BF16)
        classes.append(jnp.concatenate([d_high, d_low, f_high, f_low], axis=0))
        pieces = []
        for x in range(k + 1, k + 4):
            ref, at = (xs_ref, x) if x < STEP else (xs_next, x - STEP)
            pieces.append(ref[pl.ds(at * XS_ROW, 192), :])
        inputs.append(jnp.concatenate(pieces, axis=0))
        stacks.append(stack)

    def across(parts):
        return jnp.concatenate(parts, axis=1)

    hots = across([onehot_ref[k] for k in range(STEP)])
    acc1 = g1_ref[...] + nt(across(inputs), across(acts))
    acc2 = g2_ref[...] + nt(across(stacks), across([hidden_ref[k] for k in range(STEP)]))
    acc3 = cls_ref[...] + nt(hots, across(classes))
    g1_ref[...] = acc1
    g2_ref[...] = acc2
    cls_ref[...] = acc3

    @pl.when(step == pl.num_programs(0) - 1)
    def _():
        grads_ref[pl.ds(0, 576), :] = acc1.astype(BF16)
        grads_ref[pl.ds(576, 576), :] = (acc2 * scale).astype(BF16)
        sums = jnp.concatenate([acc3[:, :128] + acc3[:, 128:256], acc3[:, 256:384] + acc3[:, 384:]], axis=1)
        high = sums.astype(BF16)
        middle = (sums - high.astype(F32)).astype(BF16)
        low = (sums - high.astype(F32) - middle.astype(F32)).astype(BF16)
        repeat = jnp.where(iota((128, 16), 0) // 8 == iota((128, 16), 1), 1.0, 0.0).astype(BF16)
        own = iota((128, 256), 1) // 32 == iota((128, 256), 0) % 8
        row = jnp.zeros((128, 128), F32)
        for part, value in enumerate((high, middle, low)):
            fold = jnp.where(iota((256, 128), 0) % 32 + 32 * part == iota((256, 128), 1), 1.0, 0.0)
            row += dot(jnp.where(own, dot(repeat, value), 0.0).astype(BF16), fold.astype(BF16))
        row_ref[...] = row.astype(BF16)


def backward(scale, err, top, bottom, left, right, xs, first, slope, hidden, onehot, wb, gains):
    rows = err.shape[0]

    def const(shape):
        return pl.BlockSpec(shape, lambda i: (0,) * len(shape))

    def moving(shape):
        return pl.BlockSpec((STEP,) + shape[1:], lambda i: (i, 0, 0))

    def body(*refs):
        backward_body(scale, *refs)

    return pl.pallas_call(
        body,
        grid=(rows // STEP,),
        in_specs=[
            const(err.shape), const(top.shape), const(bottom.shape), const(left.shape), const(right.shape),
            pl.BlockSpec((STEP * XS_ROW, 256), lambda i: (i, 0)),
            pl.BlockSpec((STEP * XS_ROW, 256), lambda i: (i + 1, 0)), moving(first.shape), moving(slope.shape), moving(hidden.shape),
            moving(onehot.shape), const(wb.shape), const(gains.shape),
        ],
        out_specs=(const((1152, 128)), const((128, 128))),
        out_shape=(jax.ShapeDtypeStruct((1152, 128), BF16), jax.ShapeDtypeStruct((128, 128), BF16)),
        scratch_shapes=[
            pltpu.VMEM(((rows + 2) * 192, 256), BF16),
            pltpu.VMEM((576, 128), F32),
            pltpu.VMEM((576, 128), F32),
            pltpu.VMEM((16, 512), F32),
            pltpu.VMEM((128, 48), BF16),
        ],
        compiler_params=params(32),
        name="backward",
    )(err, top, bottom, left, right, *in_hbm(xs, xs, first, slope, hidden, onehot), wb, gains)


def shifts(axis):
    size = lax.axis_size(axis)
    up = [(i, i + 1) for i in range(size - 1)]
    down = [(i + 1, i) for i in range(size - 1)]
    return up, down


def row_halo(mid, width):
    up, down = shifts("wide")
    top = lax.ppermute(mid[mid.shape[0] - width :], "wide", up)
    bottom = lax.ppermute(mid[:width], "wide", down)
    return top, bottom


def column_halo(packed):
    up, down = shifts("narrow")
    left = lax.ppermute(packed[1], "narrow", up)
    right = lax.ppermute(packed[0], "narrow", down)
    return left, right


def split3(value):
    high = lax.reduce_precision(value, 8, 7)
    middle = lax.reduce_precision(value - high, 8, 7)
    low = value - high - middle
    return high.astype(BF16), middle.astype(BF16), low.astype(BF16)


def everywhere_sum(grads, parts):
    axes = ("wide", "narrow")
    n = lax.axis_size(axes)
    per = grads.shape[0] // n
    rest = parts.reshape(n, -1, 128)
    table = jnp.concatenate([grads.reshape(n, per, 128), rest], axis=1)
    got = lax.all_to_all(table, axes, 0, 0, tiled=True)
    total = got.astype(F32).sum(0)
    small = total[per:].reshape(-1, 4, 32)
    high, middle, low = split3(small.sum(1))
    small = jnp.stack([high, middle, low, jnp.zeros_like(low)], axis=1).reshape(-1, 128)
    row = jnp.concatenate([total[:per].astype(BF16), small], axis=0)
    spread = lax.all_to_all(jnp.broadcast_to(row, (n,) + row.shape), axes, 0, 0, tiled=True)
    grads = spread[:, :per].reshape(grads.shape).astype(F32)
    small = spread[:, per:].astype(F32).reshape(128, 4, 32).sum(1)
    return grads, small.reshape(16, 256)


def shards(
    teacher,
    intersection_ids,
    slot_counts,
    intersection_weights,
    student_input,
    terrain_class,
    conv_first,
    conv_second,
    class_gain,
    class_shift,
):
    band = lax.axis_index("wide")
    column = lax.axis_index("narrow")
    n_bands = lax.axis_size("wide")
    held = teacher.shape[0]
    slots = intersection_ids.shape[2]
    depth = intersection_weights.shape[1]
    rows, cols = student_input.shape[1:]

    terrain = (terrain_class + 1).astype(BF16)[:, None, :]
    mid = jnp.concatenate(
        [student_input.transpose(1, 0, 2), jnp.pad(terrain, ((0, 0), (0, CX - 65), (0, 0)))], axis=1
    )
    top, bottom = row_halo(mid, 2)
    weights = intersection_weights.reshape(-1, rows, cols)
    deep = weights.shape[0]
    cuts = (0, deep // 4, deep // 2, deep)
    parts = [rows_first(weights, x, y) for x, y in zip(cuts, cuts[1:])]
    top, bottom, parts[0] = lax.optimization_barrier((top, bottom, parts[0]))
    own = pack_columns(mid, top, bottom, 2)
    left, right = column_halo(own)

    ids = lax.dynamic_index_in_dim(intersection_ids, column, 1, keepdims=False)
    counts = lax.dynamic_index_in_dim(slot_counts, column, 1, keepdims=False)
    owner, local = ids // held, ids % held
    slot = lax.broadcasted_iota(jnp.int32, (n_bands, slots), 1)
    live = slot < counts[:, None]
    same = (owner[:, :, None] == owner[:, None, :]) & live[:, None, :]
    rank = (same & (slot[:1, None, :] < slot[:1, :, None])).sum(-1)
    which = lax.broadcasted_iota(jnp.int32, (n_bands, 2, slots), 1)
    mine = (live & (owner == band))[:, None, :] & (rank[:, None, :] == which)
    pick = (mine[..., None] & (local[:, None, :, None] == jnp.arange(held))).any(2)
    outgoing = dot(pick.reshape(2 * n_bands, held).astype(BF16), teacher).astype(BF16)
    outgoing, left, right, parts[1] = lax.optimization_barrier((outgoing, left, right, parts[1]))
    incoming = lax.all_to_all(
        outgoing.reshape(n_bands, 2, -1), "wide", split_axis=0, concat_axis=0, tiled=True
    )

    w1 = conv_first.transpose(0, 2, 3, 1).reshape(128, 576)
    w2 = conv_second.transpose(0, 2, 3, 1).reshape(64, 1152)
    wb = jnp.flip(conv_second, (2, 3)).transpose(1, 2, 3, 0).reshape(128, 576)
    gain3 = jnp.tile(class_gain.T, (1, 3))
    gs = jnp.concatenate([gain3, jnp.tile(class_shift.T, (1, 3))], axis=0)
    xs, first, slope, hidden, onehot, total = forward(mid, top, bottom, own, left, right, w1, gs, w2)

    my_owner = lax.dynamic_index_in_dim(owner, band, 0, keepdims=False)
    my_live = lax.dynamic_index_in_dim(live, band, 0, keepdims=False)
    my_rank = lax.dynamic_index_in_dim(rank, band, 0, keepdims=False)
    pair = lax.broadcasted_iota(jnp.int32, (slots, 2 * n_bands), 1)
    take = ((pair == (my_owner * 2 + my_rank)[:, None]) & my_live[:, None]).astype(BF16)
    blocks = dot(take, incoming.reshape(2 * n_bands, -1)).astype(BF16)
    blocks = blocks.reshape(slots * depth, -1).T

    err = error_rows(blocks, parts, total)
    error_field = err.transpose(1, 0, 2)
    e_top, e_bottom = row_halo(err, 1)
    e_left, e_right = column_halo(pack_columns(err, e_top, e_bottom, 1))
    scale = 1.0 / (rows * cols)
    grads, class_rows = backward(
        scale, err, e_top, e_bottom, e_left, e_right, xs, first, slope, hidden, onehot, wb, gain3
    )
    grads, classes = everywhere_sum(grads, class_rows)
    grad_first = grads[:576].reshape(3, 3, 64, 128).transpose(3, 2, 0, 1)
    grad_second = jnp.flip(grads[576:].reshape(3, 3, 64, 128), (0, 1)).transpose(2, 3, 0, 1)
    return (error_field, grad_first, grad_second, classes[:, 128:], classes[:, :128])


def solution(mesh):
    in_specs = (
        P("wide", None),
        P(),
        P(),
        P(None, None, "wide", "narrow"),
        P(None, "wide", "narrow"),
        P("wide", "narrow"),
        P(),
        P(),
        P(),
        P(),
    )
    out_specs = (P(None, "wide", "narrow"), P(), P(), P(), P())
    return jax.shard_map(shards, mesh=mesh, in_specs=in_specs, out_specs=out_specs, check_vma=False)
```

```python
import jax
import jax.numpy as jnp
from jax import lax
from jax.experimental import pallas as pl
from jax.experimental.pallas import tpu as pltpu
from jax.sharding import PartitionSpec as P

F32 = jnp.float32
BF16 = jnp.bfloat16
CX = 80


def whole():
    return pl.BlockSpec(memory_space=pltpu.VMEM)


def nt(a, b):
    return lax.dot_general(a, b, (((1,), (1,)), ((), ())), preferred_element_type=F32)


def dot(a, b):
    return jnp.dot(a, b, preferred_element_type=F32)


def iota(shape, dim):
    return lax.broadcasted_iota(jnp.int32, shape, dim)


def in_hbm(*arrays):
    return [pltpu.with_memory_space_constraint(a, pltpu.HBM) for a in arrays]


def params(mebibytes):
    return pltpu.CompilerParams(vmem_limit_bytes=mebibytes * 1024 * 1024)


def pack_columns(mid, top, bottom, width):
    rows, channels, cols = mid.shape
    span = 128 // width
    group = 8

    def body(mid_ref, top_ref, bottom_ref, out_ref):
        q = iota((cols, 256), 0)
        lane = iota((cols, 256), 1)
        part = (lane % 128) // span
        source = jnp.where(lane < 128, part, cols - width + part)
        base = jnp.where(q == source, 1.0, 0.0).astype(BF16)
        place = iota((channels, 256), 1) % span
        acc = jnp.zeros((channels, 256), F32)

        def put(acc, row, value):
            count = value.shape[0]
            picked = dot(value.reshape(count * channels, cols), base)
            for k in range(count):
                acc = jnp.where(place == row + k, picked[k * channels : (k + 1) * channels], acc)
            return acc

        acc = put(acc, 0, top_ref[...])
        acc = put(acc, width + rows, bottom_ref[...])
        for g in range(rows // group):
            acc = put(acc, width + g * group, mid_ref[pl.ds(g * group, group)])
        out_ref[0] = acc[:, :128].astype(BF16)
        out_ref[1] = acc[:, 128:].astype(BF16)

    return pl.pallas_call(
        body,
        out_shape=jax.ShapeDtypeStruct((2, channels, 128), BF16),
        in_specs=[whole()] * 3,
        out_specs=whole(),
        compiler_params=params(16),
        name="pack_columns",
    )(mid, top, bottom)


def shifted(data, halo, row):
    lane = iota(data.shape, 1)
    before = pltpu.roll(halo, (128 - row) % 128, 1)
    after = pltpu.roll(halo, (191 - row) % 128, 1)
    left = jnp.where(lane == 0, jnp.concatenate([before, before], axis=1), pltpu.roll(data, 1, 1))
    right = jnp.where(lane == 255, jnp.concatenate([after, after], axis=1), pltpu.roll(data, 255, 1))
    return left, right


XS_ROW = 208


def table_split(table):
    high = table.astype(BF16).astype(F32)
    middle = (table - high).astype(BF16).astype(F32)
    low = table - high - middle
    lane = iota(table.shape, 1)
    return jnp.where(lane < 16, high, jnp.where(lane < 32, middle, low)).astype(BF16)


def onehot_of(terrain):
    cls = jnp.broadcast_to(terrain, (16, terrain.shape[1]))
    return jnp.where(cls == (iota(cls.shape, 0) + 1).astype(F32), 1.0, 0.0).astype(BF16)


STEP = 8


def prepare_forward(
    mid_ref, top_ref, bottom_ref, own_ref, left_ref, right_ref, w1_ref, gs_ref, xs_ref, split_ref, halo_ref
):
    rows = mid_ref.shape[0]
    low_half = iota((CX, 128), 1) < 64
    left, right = left_ref[...].astype(F32), right_ref[...].astype(F32)
    own_left, own_right = own_ref[0].astype(F32), own_ref[1].astype(F32)
    near0 = jnp.where(low_half, left, own_right)
    near1 = jnp.where(low_half, pltpu.roll(left, 64, 1), pltpu.roll(right, 64, 1))
    near2 = jnp.where(low_half, own_left, right)
    halo_ref[0] = near1[:64].astype(BF16)
    halo_in = halo_ref[0]

    def build(rows_of):
        done = []
        for row, own in rows_of:
            data = own[:64]
            terrain = own[64:80].astype(F32)[0:1]
            before, after = shifted(data, halo_in, row)
            done.append((row, before, data, after, onehot_of(terrain)))
        for row, before, data, after, hot in done:
            at = row * XS_ROW if isinstance(row, int) else pl.multiple_of(row * XS_ROW, 16)
            xs_ref[pl.ds(at, 64), :] = before
            xs_ref[pl.ds(at + 64, 64), :] = data
            xs_ref[pl.ds(at + 128, 64), :] = after
            xs_ref[pl.ds(at + 192, 16), :] = hot

    build([(k, top_ref[k]) for k in range(2)] + [(rows + 2 + k, bottom_ref[k]) for k in range(2)])

    def build_mid(i, carry):
        build([(i * 4 + k + 2, mid_ref[i * 4 + k]) for k in range(4)])
        return carry

    lax.fori_loop(0, rows // 4, build_mid, 0)

    split_ref[...] = table_split(gs_ref[...])
    columns = []
    for a in range(3):
        for near in (near0, near1, near2):
            columns.append(pltpu.roll(near[:64], (128 - a) % 128, 1).astype(BF16))
    side_first = dot(w1_ref[...], jnp.concatenate(columns, axis=0))
    side_hot = onehot_of(pltpu.roll(near1[64:80], 127, 1)[0:1])
    side_pre, side_sigma = activation(split_ref[...], side_first, side_hot)
    hs_halo = (side_pre * side_sigma).astype(BF16)
    halo_ref[1] = hs_halo[:64]
    halo_ref[2] = hs_halo[64:]


def activation(split, first, hot):
    table = dot(split, jnp.concatenate([hot, hot, hot], axis=0))
    gain, shift = table[:128], table[128:]
    pre = first * gain + shift
    sigma = 1.0 / (1.0 + jnp.exp(-pre))
    return pre, sigma


def forward_body(
    mid_ref, top_ref, bottom_ref, own_ref, left_ref, right_ref, w1_ref, gs_ref, w2_ref, wb_ref, blocks_ref, weights_ref,
    xs_ref, first_ref, slope_ref, hidden_ref, onehot_ref, error_ref, wb_out, gain_out, hs_ref, split_ref, halo_ref,
):
    rows = mid_ref.shape[0]
    step = pl.program_id(0)

    @pl.when(step == 0)
    def _():
        prepare_forward(
            mid_ref, top_ref, bottom_ref, own_ref, left_ref, right_ref, w1_ref, gs_ref, xs_ref, split_ref, halo_ref
        )
        wb_out[...] = wb_ref[...]
        gain_out[...] = split_ref[pl.ds(0, 128), :]

    def activate(hs, keep):
        done = []
        split = split_ref[...]
        hidden_halo = jnp.concatenate([halo_ref[1], halo_ref[2]], axis=0)
        for h in hs:
            at = [(h + a) * XS_ROW for a in range(3)]
            if not isinstance(h, int):
                at = [pl.multiple_of(x, 16) for x in at]
            pieces = [xs_ref[pl.ds(x, 192), :] for x in at]
            first = dot(w1_ref[...], jnp.concatenate(pieces, axis=0))
            hot = xs_ref[pl.ds(at[1] + 192, 16), :]
            pre, sigma = activation(split, first, hot)
            center = (pre * sigma).astype(BF16)
            before, after = shifted(center, hidden_halo, h)
            slope = sigma * (1.0 + pre * (1.0 - sigma)) if keep else None
            done.append((h, first, slope, before, center, after, hot))
        for h, first, slope, before, center, after, hot in done:
            at = h * 384 if isinstance(h, int) else pl.multiple_of(h * 384, 16)
            hs_ref[pl.ds(at, 128), :] = before
            hs_ref[pl.ds(at + 128, 128), :] = center
            hs_ref[pl.ds(at + 256, 128), :] = after
            if keep:
                first_ref[h - 1] = first
                slope_ref[h - 1] = slope
                hidden_ref[h - 1] = center
                onehot_ref[h - 1] = hot

    @pl.when(step == 0)
    def _():
        activate([0, rows + 1], False)

    @pl.when(step < rows // STEP)
    def _():
        activate([step * STEP + k + 1 for k in range(STEP)], True)

    @pl.when(step > 0)
    def _():
        sums = []
        for k in range(STEP):
            r = (step - 1) * STEP + k
            stack = hs_ref[pl.ds(pl.multiple_of(r * 384, 16), 1152), :]
            second = dot(w2_ref[...], stack)
            target = dot(blocks_ref[...], weights_ref[k])
            sums.append((mid_ref[r][:64].astype(F32) + second - target).astype(BF16))
        for k in range(STEP):
            error_ref[(step - 1) * STEP + k] = sums[k]


def forward(mid, top, bottom, own, left, right, w1, gs, w2, wb, blocks, weights):
    rows = mid.shape[0]
    return pl.pallas_call(
        forward_body,
        grid=(rows // STEP + 1,),
        out_shape=(
            pltpu.VMEM(((rows + 4) * XS_ROW, 256), BF16),
            pltpu.VMEM((rows, 128, 256), F32),
            pltpu.VMEM((rows, 128, 256), F32),
            pltpu.VMEM((rows, 128, 256), BF16),
            pltpu.VMEM((rows, 16, 256), BF16),
            pltpu.VMEM((rows, 64, 256), BF16),
            pltpu.VMEM((128, 576), BF16),
            pltpu.VMEM((128, 48), BF16),
        ),
        in_specs=[whole()] * 11
        + [pl.BlockSpec((STEP,) + weights.shape[1:], lambda i: (jnp.maximum(i - 1, 0), 0, 0))],
        out_specs=(whole(),) * 8,
        scratch_shapes=[
            pltpu.VMEM(((rows + 2) * 384, 256), BF16),
            pltpu.VMEM((256, 48), BF16),
            pltpu.VMEM((3, 64, 128), BF16),
        ],
        compiler_params=params(26),
        name="forward",
    )(mid, top, bottom, own, left, right, w1, gs, w2, wb, blocks, *in_hbm(weights))


def rows_first(weights, start, stop):
    rows, cols = weights.shape[1:]
    chunk = 128

    def body(in_ref, out_ref):
        out_ref[...] = jnp.swapaxes(in_ref[...], 0, 1)

    return pl.pallas_call(
        body,
        grid=((stop - start) // chunk,),
        in_specs=[pl.BlockSpec((chunk, rows, cols), lambda i: (i + start // chunk, 0, 0))],
        out_specs=pl.BlockSpec((rows, chunk, cols), lambda i: (0, i, 0)),
        out_shape=pltpu.HBM((rows, stop - start, cols), BF16),
        compiler_params=params(14),
        name="rows_first",
    )(*in_hbm(weights))


def backward_body(
    scale, err_ref, top_ref, bottom_ref, left_ref, right_ref, xs_ref, first_ref, slope_ref,
    hidden_ref, onehot_ref, wb_ref, gain_ref, grads_ref, row_ref, es_ref, g1_ref, g2_ref, cls_ref,
):
    rows = err_ref.shape[0]
    step = pl.program_id(0)

    @pl.when(step == 0)
    def _():
        left, right = left_ref[...].astype(F32), right_ref[...].astype(F32)
        halo = jnp.where(iota(left.shape, 1) < 64, left, pltpu.roll(right, 64, 1)).astype(BF16)

        def build(rows_of):
            done = [(row, own, shifted(own, halo, row)) for row, own in rows_of]
            for row, own, (before, after) in done:
                at = row * 192
                es_ref[pl.ds(at, 64), :] = before
                es_ref[pl.ds(at + 64, 64), :] = own
                es_ref[pl.ds(at + 128, 64), :] = after

        build([(0, top_ref[0]), (rows + 1, bottom_ref[0])])
        for r in range(0, rows, 4):
            build([(r + k + 1, err_ref[r + k]) for k in range(4)])
        g1_ref[...] = jnp.zeros_like(g1_ref)
        g2_ref[...] = jnp.zeros_like(g2_ref)
        cls_ref[...] = jnp.zeros_like(cls_ref)

    split = gain_ref[...]
    stacks, acts, inputs, classes = [], [], [], []
    for k in range(STEP):
        r = step * STEP + k
        stack = es_ref[pl.ds(pl.multiple_of(r * 192, 16), 576), :]
        back = dot(wb_ref[...], stack)
        delta = back * slope_ref[r] * scale
        hot = onehot_ref[r]
        gain = dot(split, jnp.concatenate([hot, hot, hot], axis=0))
        acts.append((delta * gain).astype(BF16))
        scaled_first = delta * first_ref[r]
        d_high = delta.astype(BF16)
        d_low = (delta - d_high.astype(F32)).astype(BF16)
        f_high = scaled_first.astype(BF16)
        f_low = (scaled_first - f_high.astype(F32)).astype(BF16)
        classes.append(jnp.concatenate([d_high, d_low, f_high, f_low], axis=0))
        pieces = [xs_ref[pl.ds(pl.multiple_of((r + 1 + x) * XS_ROW, 16), 192), :] for x in range(3)]
        inputs.append(jnp.concatenate(pieces, axis=0))
        stacks.append(stack)

    def across(parts):
        return jnp.concatenate(parts, axis=1)

    hots = across([onehot_ref[step * STEP + k] for k in range(STEP)])
    acc1 = g1_ref[...] + nt(across(inputs), across(acts))
    acc2 = g2_ref[...] + nt(across(stacks), across([hidden_ref[step * STEP + k] for k in range(STEP)]))
    acc3 = cls_ref[...] + nt(hots, across(classes))
    g1_ref[...] = acc1
    g2_ref[...] = acc2
    cls_ref[...] = acc3

    @pl.when(step == pl.num_programs(0) - 1)
    def _():
        grads_ref[pl.ds(0, 576), :] = acc1.astype(BF16)
        grads_ref[pl.ds(576, 576), :] = (acc2 * scale).astype(BF16)
        sums = jnp.concatenate([acc3[:, :128] + acc3[:, 128:256], acc3[:, 256:384] + acc3[:, 384:]], axis=1)
        high = sums.astype(BF16)
        middle = (sums - high.astype(F32)).astype(BF16)
        low = (sums - high.astype(F32) - middle.astype(F32)).astype(BF16)
        repeat = jnp.where(iota((128, 16), 0) // 8 == iota((128, 16), 1), 1.0, 0.0).astype(BF16)
        own = iota((128, 256), 1) // 32 == iota((128, 256), 0) % 8
        row = jnp.zeros((128, 128), F32)
        for part, value in enumerate((high, middle, low)):
            fold = jnp.where(iota((256, 128), 0) % 32 + 32 * part == iota((256, 128), 1), 1.0, 0.0)
            row += dot(jnp.where(own, dot(repeat, value), 0.0).astype(BF16), fold.astype(BF16))
        row_ref[...] = row.astype(BF16)


def backward(scale, err, top, bottom, left, right, xs, first, slope, hidden, onehot, wb, gains):
    rows = err.shape[0]

    def const(shape):
        return pl.BlockSpec(shape, lambda i: (0,) * len(shape))

    def body(*refs):
        backward_body(scale, *refs)

    return pl.pallas_call(
        body,
        grid=(rows // STEP,),
        in_specs=[whole()] * 12,
        out_specs=(const((1152, 128)), const((128, 128))),
        out_shape=(jax.ShapeDtypeStruct((1152, 128), BF16), jax.ShapeDtypeStruct((128, 128), BF16)),
        scratch_shapes=[
            pltpu.VMEM(((rows + 2) * 192, 256), BF16),
            pltpu.VMEM((576, 128), F32),
            pltpu.VMEM((576, 128), F32),
            pltpu.VMEM((16, 512), F32),
        ],
        compiler_params=params(14),
        name="backward",
    )(err, top, bottom, left, right, xs, first, slope, hidden, onehot, wb, gains)


def shifts(axis):
    size = lax.axis_size(axis)
    up = [(i, i + 1) for i in range(size - 1)]
    down = [(i + 1, i) for i in range(size - 1)]
    return up, down


def row_halo(mid, width):
    up, down = shifts("wide")
    top = lax.ppermute(mid[mid.shape[0] - width :], "wide", up)
    bottom = lax.ppermute(mid[:width], "wide", down)
    return top, bottom


def column_halo(packed):
    up, down = shifts("narrow")
    left = lax.ppermute(packed[1], "narrow", up)
    right = lax.ppermute(packed[0], "narrow", down)
    return left, right


def split3(value):
    high = lax.reduce_precision(value, 8, 7)
    middle = lax.reduce_precision(value - high, 8, 7)
    low = value - high - middle
    return high.astype(BF16), middle.astype(BF16), low.astype(BF16)


def everywhere_sum(grads, parts):
    axes = ("wide", "narrow")
    n = lax.axis_size(axes)
    per = grads.shape[0] // n
    rest = parts.reshape(n, -1, 128)
    table = jnp.concatenate([grads.reshape(n, per, 128), rest], axis=1)
    got = lax.all_to_all(table, axes, 0, 0, tiled=True)
    total = got.astype(F32).sum(0)
    small = total[per:].reshape(-1, 4, 32)
    high, middle, low = split3(small.sum(1))
    small = jnp.stack([high, middle, low, jnp.zeros_like(low)], axis=1).reshape(-1, 128)
    row = jnp.concatenate([total[:per].astype(BF16), small], axis=0)
    spread = lax.all_to_all(jnp.broadcast_to(row, (n,) + row.shape), axes, 0, 0, tiled=True)
    grads = spread[:, :per].reshape(grads.shape).astype(F32)
    small = spread[:, per:].astype(F32).reshape(128, 4, 32).sum(1)
    return grads, small.reshape(16, 256)


def shards(
    teacher,
    intersection_ids,
    slot_counts,
    intersection_weights,
    student_input,
    terrain_class,
    conv_first,
    conv_second,
    class_gain,
    class_shift,
):
    band = lax.axis_index("wide")
    column = lax.axis_index("narrow")
    n_bands = lax.axis_size("wide")
    held = teacher.shape[0]
    slots = intersection_ids.shape[2]
    depth = intersection_weights.shape[1]
    rows, cols = student_input.shape[1:]

    terrain = (terrain_class + 1).astype(BF16)[:, None, :]
    mid = jnp.concatenate(
        [student_input.transpose(1, 0, 2), jnp.pad(terrain, ((0, 0), (0, CX - 65), (0, 0)))], axis=1
    )
    top, bottom = row_halo(mid, 2)
    weights = intersection_weights.reshape(-1, rows, cols)
    weights = rows_first(weights, 0, weights.shape[0])
    own = pack_columns(mid, top, bottom, 2)
    own, weights = lax.optimization_barrier((own, weights))
    left, right = column_halo(own)

    ids = lax.dynamic_index_in_dim(intersection_ids, column, 1, keepdims=False)
    counts = lax.dynamic_index_in_dim(slot_counts, column, 1, keepdims=False)
    owner, local = ids // held, ids % held
    slot = lax.broadcasted_iota(jnp.int32, (n_bands, slots), 1)
    live = slot < counts[:, None]
    same = (owner[:, :, None] == owner[:, None, :]) & live[:, None, :]
    rank = (same & (slot[:1, None, :] < slot[:1, :, None])).sum(-1)
    which = lax.broadcasted_iota(jnp.int32, (n_bands, 2, slots), 1)
    mine = (live & (owner == band))[:, None, :] & (rank[:, None, :] == which)
    pick = (mine[..., None] & (local[:, None, :, None] == jnp.arange(held))).any(2)
    outgoing = dot(pick.reshape(2 * n_bands, held).astype(BF16), teacher).astype(BF16)
    incoming = lax.all_to_all(
        outgoing.reshape(n_bands, 2, -1), "wide", split_axis=0, concat_axis=0, tiled=True
    )

    w1 = conv_first.transpose(0, 2, 3, 1).reshape(128, 576)
    w2 = conv_second.transpose(0, 2, 3, 1).reshape(64, 1152)
    wb = jnp.flip(conv_second, (2, 3)).transpose(1, 2, 3, 0).reshape(128, 576)
    gain3 = jnp.tile(class_gain.T, (1, 3))
    gs = jnp.concatenate([gain3, jnp.tile(class_shift.T, (1, 3))], axis=0)

    my_owner = lax.dynamic_index_in_dim(owner, band, 0, keepdims=False)
    my_live = lax.dynamic_index_in_dim(live, band, 0, keepdims=False)
    my_rank = lax.dynamic_index_in_dim(rank, band, 0, keepdims=False)
    pair = lax.broadcasted_iota(jnp.int32, (slots, 2 * n_bands), 1)
    take = ((pair == (my_owner * 2 + my_rank)[:, None]) & my_live[:, None]).astype(BF16)
    blocks = dot(take, incoming.reshape(2 * n_bands, -1)).astype(BF16)
    blocks = blocks.reshape(slots * depth, -1).T

    xs, first, slope, hidden, onehot, err, wb, gains = forward(
        mid, top, bottom, own, left, right, w1, gs, w2, wb, blocks, weights
    )
    error_field = err.transpose(1, 0, 2)
    e_top, e_bottom = row_halo(err, 1)
    e_left, e_right = column_halo(pack_columns(err, e_top, e_bottom, 1))
    scale = 1.0 / (rows * cols)
    grads, class_rows = backward(
        scale, err, e_top, e_bottom, e_left, e_right, xs, first, slope, hidden, onehot, wb, gains
    )
    grads, classes = everywhere_sum(grads, class_rows)
    grad_first = grads[:576].reshape(3, 3, 64, 128).transpose(3, 2, 0, 1)
    grad_second = jnp.flip(grads[576:].reshape(3, 3, 64, 128), (0, 1)).transpose(2, 3, 0, 1)
    return (error_field, grad_first, grad_second, classes[:, 128:], classes[:, :128])


def solution(mesh):
    in_specs = (
        P("wide", None),
        P(),
        P(),
        P(None, None, "wide", "narrow"),
        P(None, "wide", "narrow"),
        P("wide", "narrow"),
        P(),
        P(),
        P(),
        P(),
    )
    out_specs = (P(None, "wide", "narrow"), P(), P(), P(), P())
    return jax.shard_map(shards, mesh=mesh, in_specs=in_specs, out_specs=out_specs, check_vma=False)
```

```python
import jax
import jax.numpy as jnp
from jax import lax
from jax.experimental import pallas as pl
from jax.experimental.pallas import tpu as pltpu
from jax.sharding import PartitionSpec as P

F32 = jnp.float32
BF16 = jnp.bfloat16
CX = 80


def whole():
    return pl.BlockSpec(memory_space=pltpu.VMEM)


def nt(a, b):
    return lax.dot_general(a, b, (((1,), (1,)), ((), ())), preferred_element_type=F32)


def dot(a, b):
    return jnp.dot(a, b, preferred_element_type=F32)


def iota(shape, dim):
    return lax.broadcasted_iota(jnp.int32, shape, dim)


def in_hbm(*arrays):
    return [pltpu.with_memory_space_constraint(a, pltpu.HBM) for a in arrays]


def params(mebibytes):
    return pltpu.CompilerParams(vmem_limit_bytes=mebibytes * 1024 * 1024)


def pack_columns(mid, top, bottom, width):
    rows, channels, cols = mid.shape
    span = 128 // width
    group = 8

    def body(mid_ref, top_ref, bottom_ref, out_ref):
        q = iota((cols, 256), 0)
        lane = iota((cols, 256), 1)
        part = (lane % 128) // span
        source = jnp.where(lane < 128, part, cols - width + part)
        base = jnp.where(q == source, 1.0, 0.0).astype(BF16)
        place = iota((channels, 256), 1) % span
        acc = jnp.zeros((channels, 256), F32)

        def put(acc, row, value):
            count = value.shape[0]
            picked = dot(value.reshape(count * channels, cols), base)
            for k in range(count):
                acc = jnp.where(place == row + k, picked[k * channels : (k + 1) * channels], acc)
            return acc

        acc = put(acc, 0, top_ref[...])
        acc = put(acc, width + rows, bottom_ref[...])
        for g in range(rows // group):
            acc = put(acc, width + g * group, mid_ref[pl.ds(g * group, group)])
        out_ref[0] = acc[:, :128].astype(BF16)
        out_ref[1] = acc[:, 128:].astype(BF16)

    return pl.pallas_call(
        body,
        out_shape=jax.ShapeDtypeStruct((2, channels, 128), BF16),
        in_specs=[whole()] * 3,
        out_specs=whole(),
        compiler_params=params(16),
        name="pack_columns",
    )(mid, top, bottom)


def shifted(data, halo, row):
    lane = iota(data.shape, 1)
    before = pltpu.roll(halo, (128 - row) % 128, 1)
    after = pltpu.roll(halo, (191 - row) % 128, 1)
    left = jnp.where(lane == 0, jnp.concatenate([before, before], axis=1), pltpu.roll(data, 1, 1))
    right = jnp.where(lane == 255, jnp.concatenate([after, after], axis=1), pltpu.roll(data, 255, 1))
    return left, right


XS_ROW = 208


def table_split(table):
    high = table.astype(BF16).astype(F32)
    middle = (table - high).astype(BF16).astype(F32)
    low = table - high - middle
    lane = iota(table.shape, 1)
    return jnp.where(lane < 16, high, jnp.where(lane < 32, middle, low)).astype(BF16)


def onehot_of(terrain):
    cls = jnp.broadcast_to(terrain, (16, terrain.shape[1]))
    return jnp.where(cls == (iota(cls.shape, 0) + 1).astype(F32), 1.0, 0.0).astype(BF16)


STEP = 8


def prepare_forward(
    mid_ref, top_ref, bottom_ref, own_ref, left_ref, right_ref, w1_ref, gs_ref, xs_ref, split_ref, halo_ref
):
    rows = mid_ref.shape[0]
    low_half = iota((CX, 128), 1) < 64
    left, right = left_ref[...].astype(F32), right_ref[...].astype(F32)
    own_left, own_right = own_ref[0].astype(F32), own_ref[1].astype(F32)
    near0 = jnp.where(low_half, left, own_right)
    near1 = jnp.where(low_half, pltpu.roll(left, 64, 1), pltpu.roll(right, 64, 1))
    near2 = jnp.where(low_half, own_left, right)
    halo_ref[0] = near1[:64].astype(BF16)
    halo_in = halo_ref[0]

    def build(rows_of):
        done = []
        for row, own in rows_of:
            data = own[:64]
            terrain = own[64:80].astype(F32)[0:1]
            before, after = shifted(data, halo_in, row)
            done.append((row, before, data, after, onehot_of(terrain)))
        for row, before, data, after, hot in done:
            at = row * XS_ROW if isinstance(row, int) else pl.multiple_of(row * XS_ROW, 16)
            xs_ref[pl.ds(at, 64), :] = before
            xs_ref[pl.ds(at + 64, 64), :] = data
            xs_ref[pl.ds(at + 128, 64), :] = after
            xs_ref[pl.ds(at + 192, 16), :] = hot

    build([(k, top_ref[k]) for k in range(2)] + [(rows + 2 + k, bottom_ref[k]) for k in range(2)])

    def build_mid(i, carry):
        build([(i * 4 + k + 2, mid_ref[i * 4 + k]) for k in range(4)])
        return carry

    lax.fori_loop(0, rows // 4, build_mid, 0)

    split_ref[...] = table_split(gs_ref[...])
    columns = []
    for a in range(3):
        for near in (near0, near1, near2):
            columns.append(pltpu.roll(near[:64], (128 - a) % 128, 1).astype(BF16))
    side_first = dot(w1_ref[...], jnp.concatenate(columns, axis=0))
    side_hot = onehot_of(pltpu.roll(near1[64:80], 127, 1)[0:1])
    side_pre, side_sigma = activation(split_ref[...], side_first, side_hot)
    hs_halo = (side_pre * side_sigma).astype(BF16)
    halo_ref[1] = hs_halo[:64]
    halo_ref[2] = hs_halo[64:]


def activation(split, first, hot):
    table = dot(split, jnp.concatenate([hot, hot, hot], axis=0))
    gain, shift = table[:128], table[128:]
    pre = first * gain + shift
    sigma = 1.0 / (1.0 + jnp.exp(-pre))
    return pre, sigma


def forward_body(
    mid_ref, top_ref, bottom_ref, own_ref, left_ref, right_ref, w1_ref, gs_ref, w2_ref, wb_ref, blocks_ref, weights_ref,
    xs_ref, first_ref, slope_ref, hidden_ref, onehot_ref, error_ref, wb_out, gain_out, hs_ref, split_ref, halo_ref,
):
    rows = mid_ref.shape[0]
    step = pl.program_id(0)

    @pl.when(step == 0)
    def _():
        prepare_forward(
            mid_ref, top_ref, bottom_ref, own_ref, left_ref, right_ref, w1_ref, gs_ref, xs_ref, split_ref, halo_ref
        )
        wb_out[...] = wb_ref[...]
        gain_out[...] = split_ref[pl.ds(0, 128), :]

    def activate(hs, keep):
        done = []
        split = split_ref[...]
        hidden_halo = jnp.concatenate([halo_ref[1], halo_ref[2]], axis=0)
        for h in hs:
            at = [(h + a) * XS_ROW for a in range(3)]
            if not isinstance(h, int):
                at = [pl.multiple_of(x, 16) for x in at]
            pieces = [xs_ref[pl.ds(x, 192), :] for x in at]
            first = dot(w1_ref[...], jnp.concatenate(pieces, axis=0))
            hot = xs_ref[pl.ds(at[1] + 192, 16), :]
            pre, sigma = activation(split, first, hot)
            center = (pre * sigma).astype(BF16)
            before, after = shifted(center, hidden_halo, h)
            slope = sigma * (1.0 + pre * (1.0 - sigma)) if keep else None
            done.append((h, first, slope, before, center, after, hot))
        for h, first, slope, before, center, after, hot in done:
            at = h * 384 if isinstance(h, int) else pl.multiple_of(h * 384, 16)
            hs_ref[pl.ds(at, 128), :] = before
            hs_ref[pl.ds(at + 128, 128), :] = center
            hs_ref[pl.ds(at + 256, 128), :] = after
            if keep:
                first_ref[h - 1] = first
                slope_ref[h - 1] = slope
                hidden_ref[h - 1] = center
                onehot_ref[h - 1] = hot

    @pl.when(step == 0)
    def _():
        activate([0, rows + 1], False)

    @pl.when(step < rows // STEP)
    def _():
        activate([step * STEP + k + 1 for k in range(STEP)], True)

    @pl.when(step > 0)
    def _():
        sums = []
        for k in range(STEP):
            r = (step - 1) * STEP + k
            stack = hs_ref[pl.ds(pl.multiple_of(r * 384, 16), 1152), :]
            second = dot(w2_ref[...], stack)
            target = dot(blocks_ref[...], weights_ref[k])
            sums.append((mid_ref[r][:64].astype(F32) + second - target).astype(BF16))
        for k in range(STEP):
            error_ref[(step - 1) * STEP + k] = sums[k]


def forward(mid, top, bottom, own, left, right, w1, gs, w2, wb, blocks, weights):
    rows = mid.shape[0]
    return pl.pallas_call(
        forward_body,
        grid=(rows // STEP + 1,),
        out_shape=(
            pltpu.VMEM(((rows + 4) * XS_ROW, 256), BF16),
            pltpu.VMEM((rows, 128, 256), F32),
            pltpu.VMEM((rows, 128, 256), F32),
            pltpu.VMEM((rows, 128, 256), BF16),
            pltpu.VMEM((rows, 16, 256), BF16),
            pltpu.VMEM((rows, 64, 256), BF16),
            pltpu.VMEM((128, 576), BF16),
            pltpu.VMEM((128, 48), BF16),
        ),
        in_specs=[whole()] * 11
        + [pl.BlockSpec((STEP,) + weights.shape[1:], lambda i: (jnp.maximum(i - 1, 0), 0, 0))],
        out_specs=(whole(),) * 8,
        scratch_shapes=[
            pltpu.VMEM(((rows + 2) * 384, 256), BF16),
            pltpu.VMEM((256, 48), BF16),
            pltpu.VMEM((3, 64, 128), BF16),
        ],
        compiler_params=params(26),
        name="forward",
    )(mid, top, bottom, own, left, right, w1, gs, w2, wb, blocks, *in_hbm(weights))


def rows_first(weights, start, stop):
    rows, cols = weights.shape[1:]
    chunk = 128

    def body(in_ref, out_ref):
        out_ref[...] = jnp.swapaxes(in_ref[...], 0, 1)

    return pl.pallas_call(
        body,
        grid=((stop - start) // chunk,),
        in_specs=[pl.BlockSpec((chunk, rows, cols), lambda i: (i + start // chunk, 0, 0))],
        out_specs=pl.BlockSpec((rows, chunk, cols), lambda i: (0, i, 0)),
        out_shape=pltpu.HBM((rows, stop - start, cols), BF16),
        compiler_params=params(14),
        name="rows_first",
    )(*in_hbm(weights))


def backward_body(
    scale, err_ref, top_ref, bottom_ref, left_ref, right_ref, xs_ref, first_ref, slope_ref,
    hidden_ref, onehot_ref, wb_ref, gain_ref, grads_ref, row_ref, es_ref, g1_ref, g2_ref, cls_ref,
):
    rows = err_ref.shape[0]
    step = pl.program_id(0)

    @pl.when(step == 0)
    def _():
        left, right = left_ref[...].astype(F32), right_ref[...].astype(F32)
        halo = jnp.where(iota(left.shape, 1) < 64, left, pltpu.roll(right, 64, 1)).astype(BF16)

        def build(rows_of):
            done = [(row, own, shifted(own, halo, row)) for row, own in rows_of]
            for row, own, (before, after) in done:
                at = row * 192
                es_ref[pl.ds(at, 64), :] = before
                es_ref[pl.ds(at + 64, 64), :] = own
                es_ref[pl.ds(at + 128, 64), :] = after

        build([(0, top_ref[0]), (rows + 1, bottom_ref[0])])
        for r in range(0, rows, 4):
            build([(r + k + 1, err_ref[r + k]) for k in range(4)])
        g1_ref[...] = jnp.zeros_like(g1_ref)
        g2_ref[...] = jnp.zeros_like(g2_ref)
        cls_ref[...] = jnp.zeros_like(cls_ref)

    split = gain_ref[...]
    stacks, acts, inputs, classes = [], [], [], []
    for k in range(STEP):
        r = step * STEP + k
        stack = es_ref[pl.ds(pl.multiple_of(r * 192, 16), 576), :]
        back = dot(wb_ref[...], stack)
        delta = back * slope_ref[r] * scale
        hot = onehot_ref[r]
        gain = dot(split, jnp.concatenate([hot, hot, hot], axis=0))
        acts.append((delta * gain).astype(BF16))
        scaled_first = delta * first_ref[r]
        d_high = delta.astype(BF16)
        d_low = (delta - d_high.astype(F32)).astype(BF16)
        f_high = scaled_first.astype(BF16)
        f_low = (scaled_first - f_high.astype(F32)).astype(BF16)
        classes.append(jnp.concatenate([d_high, d_low, f_high, f_low], axis=0))
        pieces = [xs_ref[pl.ds(pl.multiple_of((r + 1 + x) * XS_ROW, 16), 192), :] for x in range(3)]
        inputs.append(jnp.concatenate(pieces, axis=0))
        stacks.append(stack)

    def across(parts):
        return jnp.concatenate(parts, axis=1)

    hots = across([onehot_ref[step * STEP + k] for k in range(STEP)])
    acc1 = g1_ref[...] + nt(across(inputs), across(acts))
    acc2 = g2_ref[...] + nt(across(stacks), across([hidden_ref[step * STEP + k] for k in range(STEP)]))
    acc3 = cls_ref[...] + nt(hots, across(classes))
    g1_ref[...] = acc1
    g2_ref[...] = acc2
    cls_ref[...] = acc3

    @pl.when(step == pl.num_programs(0) - 1)
    def _():
        grads_ref[pl.ds(0, 576), :] = acc1.astype(BF16)
        grads_ref[pl.ds(576, 576), :] = (acc2 * scale).astype(BF16)
        sums = jnp.concatenate([acc3[:, :128] + acc3[:, 128:256], acc3[:, 256:384] + acc3[:, 384:]], axis=1)
        high = sums.astype(BF16)
        middle = (sums - high.astype(F32)).astype(BF16)
        low = (sums - high.astype(F32) - middle.astype(F32)).astype(BF16)
        repeat = jnp.where(iota((128, 16), 0) // 8 == iota((128, 16), 1), 1.0, 0.0).astype(BF16)
        own = iota((128, 256), 1) // 32 == iota((128, 256), 0) % 8
        row = jnp.zeros((128, 128), F32)
        for part, value in enumerate((high, middle, low)):
            fold = jnp.where(iota((256, 128), 0) % 32 + 32 * part == iota((256, 128), 1), 1.0, 0.0)
            row += dot(jnp.where(own, dot(repeat, value), 0.0).astype(BF16), fold.astype(BF16))
        row_ref[...] = row.astype(BF16)


def backward(scale, err, top, bottom, left, right, xs, first, slope, hidden, onehot, wb, gains):
    rows = err.shape[0]

    def const(shape):
        return pl.BlockSpec(shape, lambda i: (0,) * len(shape))

    def body(*refs):
        backward_body(scale, *refs)

    return pl.pallas_call(
        body,
        grid=(rows // STEP,),
        in_specs=[whole()] * 12,
        out_specs=(const((1152, 128)), const((128, 128))),
        out_shape=(jax.ShapeDtypeStruct((1152, 128), BF16), jax.ShapeDtypeStruct((128, 128), BF16)),
        scratch_shapes=[
            pltpu.VMEM(((rows + 2) * 192, 256), BF16),
            pltpu.VMEM((576, 128), F32),
            pltpu.VMEM((576, 128), F32),
            pltpu.VMEM((16, 512), F32),
        ],
        compiler_params=params(14),
        name="backward",
    )(err, top, bottom, left, right, xs, first, slope, hidden, onehot, wb, gains)


def shifts(axis):
    size = lax.axis_size(axis)
    up = [(i, i + 1) for i in range(size - 1)]
    down = [(i + 1, i) for i in range(size - 1)]
    return up, down


def row_halo(mid, width):
    up, down = shifts("wide")
    top = lax.ppermute(mid[mid.shape[0] - width :], "wide", up)
    bottom = lax.ppermute(mid[:width], "wide", down)
    return top, bottom


def column_halo(packed):
    up, down = shifts("narrow")
    left = lax.ppermute(packed[1], "narrow", up)
    right = lax.ppermute(packed[0], "narrow", down)
    return left, right


def split3(value):
    high = lax.reduce_precision(value, 8, 7)
    middle = lax.reduce_precision(value - high, 8, 7)
    low = value - high - middle
    return high.astype(BF16), middle.astype(BF16), low.astype(BF16)


def everywhere_sum(grads, parts):
    axes = ("wide", "narrow")
    n = lax.axis_size(axes)
    per = grads.shape[0] // n
    rest = parts.reshape(n, -1, 128)
    table = jnp.concatenate([grads.reshape(n, per, 128), rest], axis=1)
    got = lax.all_to_all(table, axes, 0, 0, tiled=True)
    total = got.astype(F32).sum(0)
    small = total[per:].reshape(-1, 4, 32)
    high, middle, low = split3(small.sum(1))
    small = jnp.stack([high, middle, low, jnp.zeros_like(low)], axis=1).reshape(-1, 128)
    row = jnp.concatenate([total[:per].astype(BF16), small], axis=0)
    spread = lax.all_to_all(jnp.broadcast_to(row, (n,) + row.shape), axes, 0, 0, tiled=True)
    grads = spread[:, :per].reshape(grads.shape).astype(F32)
    small = spread[:, per:].astype(F32).reshape(128, 4, 32).sum(1)
    return grads, small.reshape(16, 256)


def shards(
    teacher,
    intersection_ids,
    slot_counts,
    intersection_weights,
    student_input,
    terrain_class,
    conv_first,
    conv_second,
    class_gain,
    class_shift,
):
    band = lax.axis_index("wide")
    column = lax.axis_index("narrow")
    n_bands = lax.axis_size("wide")
    held = teacher.shape[0]
    slots = intersection_ids.shape[2]
    depth = intersection_weights.shape[1]
    rows, cols = student_input.shape[1:]

    terrain = (terrain_class + 1).astype(BF16)[:, None, :]
    mid = jnp.concatenate(
        [student_input.transpose(1, 0, 2), jnp.pad(terrain, ((0, 0), (0, CX - 65), (0, 0)))], axis=1
    )
    top, bottom = row_halo(mid, 2)
    weights = intersection_weights.reshape(-1, rows, cols)
    weights = rows_first(weights, 0, weights.shape[0])
    own = pack_columns(mid, top, bottom, 2)
    own, weights = lax.optimization_barrier((own, weights))
    left, right = column_halo(own)

    ids = lax.dynamic_index_in_dim(intersection_ids, column, 1, keepdims=False)
    counts = lax.dynamic_index_in_dim(slot_counts, column, 1, keepdims=False)
    slot = lax.broadcasted_iota(jnp.int32, (n_bands, slots), 1)
    mine = (slot < counts[:, None]) & (lax.div(ids, held) == band)
    code = slot * held + lax.rem(ids, held)
    last = slots * held
    early = jnp.where(mine, code, last).min(1)
    late = jnp.where(mine, code, -1).max(1)
    picked = jnp.stack(
        [jnp.where(early < last, lax.rem(early, held), -1), jnp.where(late > early, lax.rem(late, held), -1)], axis=1
    )
    pick = (picked[:, :, None] == jnp.arange(held)).astype(BF16)
    outgoing = dot(pick.reshape(2 * n_bands, held), teacher).astype(BF16)
    incoming = lax.all_to_all(
        outgoing.reshape(n_bands, 2, -1), "wide", split_axis=0, concat_axis=0, tiled=True
    )

    w1 = conv_first.transpose(0, 2, 3, 1).reshape(128, 576)
    w2 = conv_second.transpose(0, 2, 3, 1).reshape(64, 1152)
    wb = jnp.flip(conv_second, (2, 3)).transpose(1, 2, 3, 0).reshape(128, 576)
    gain3 = jnp.tile(class_gain.T, (1, 3))
    gs = jnp.concatenate([gain3, jnp.tile(class_shift.T, (1, 3))], axis=0)

    here = jnp.arange(n_bands) == band
    my_owner = lax.div(jnp.where(here[:, None], ids, 0).sum(0), held)
    my_slot = jnp.arange(slots)
    my_live = my_slot < jnp.where(here, counts, 0).sum()
    same = (my_owner[:, None] == my_owner[None, :]) & my_live[None, :]
    my_rank = (same & (my_slot[None, :] < my_slot[:, None])).sum(1)
    pair = lax.broadcasted_iota(jnp.int32, (slots, 2 * n_bands), 1)
    take = ((pair == (my_owner * 2 + my_rank)[:, None]) & my_live[:, None]).astype(BF16)
    blocks = dot(take, incoming.reshape(2 * n_bands, -1)).astype(BF16)
    blocks = blocks.reshape(slots * depth, -1).T

    xs, first, slope, hidden, onehot, err, wb, gains = forward(
        mid, top, bottom, own, left, right, w1, gs, w2, wb, blocks, weights
    )
    error_field = err.transpose(1, 0, 2)
    e_top, e_bottom = row_halo(err, 1)
    e_left, e_right = column_halo(pack_columns(err, e_top, e_bottom, 1))
    scale = 1.0 / (rows * cols)
    grads, class_rows = backward(
        scale, err, e_top, e_bottom, e_left, e_right, xs, first, slope, hidden, onehot, wb, gains
    )
    grads, classes = everywhere_sum(grads, class_rows)
    grad_first = grads[:576].reshape(3, 3, 64, 128).transpose(3, 2, 0, 1)
    grad_second = jnp.flip(grads[576:].reshape(3, 3, 64, 128), (0, 1)).transpose(2, 3, 0, 1)
    return (error_field, grad_first, grad_second, classes[:, 128:], classes[:, :128])


def solution(mesh):
    in_specs = (
        P("wide", None),
        P(),
        P(),
        P(None, None, "wide", "narrow"),
        P(None, "wide", "narrow"),
        P("wide", "narrow"),
        P(),
        P(),
        P(),
        P(),
    )
    out_specs = (P(None, "wide", "narrow"), P(), P(), P(), P())
    return jax.shard_map(shards, mesh=mesh, in_specs=in_specs, out_specs=out_specs, check_vma=False)
```
